256 devices in a mesh: group: 16 (over z, core), member: 16 (over x, y).
Axes of the slice: x: 4, y: 4, z: 8, core: 2. Of those that a mesh axis runs over, the one named last changes fastest.
Arguments:
- features: float32 [98304, 256], P(('group', 'member')), may hold values from 0.01 to 9
- tiles: float32 [24576, 128, 128], P(('group', 'member')), may hold values from 0 to 1.5, as said below
- tile_col: int32 [24576], P(('group', 'member')), may hold values from 0 to 47
- tile_slot: int32 [24576], P(('group', 'member')), may hold values from 0 to 31
- mirror_list: int32 [256, 16, 2], P(('group', 'member')), may hold values from 0 to 2, as said below
- tile_counts: int32 [256], P(('group', 'member')), may hold values from 64 to 96, as said below
- self_weight: float32 [2, 256, 256], replicated, may hold values from -0.375 to 0.375
- neigh_weight: float32 [2, 256, 256], replicated, may hold values from -0.375 to 0.375
Outputs:
- embeddings: float32 [98304, 256], P(('group', 'member'))
The draws below stay inside these ranges and needn't reach their ends.
Inputs may be any that keep to these rules, and one draw needn't show every extreme that they name: `tiles`: positive edge weights. `tile_col`: an index among the 48 blocks of the tile's group. `tile_slot`: an index among the device's 32 mirror slots. `mirror_list`: the 2 entries of one device and one destination group differ. `tile_counts`: some device has all 96 tiles live.
All inputs are finite; a program needn't handle non-finite values.
Results may differ from the reference program's by a relative error of at most 0.0003.
Values sent between devices are 32-bit elements; how exact they have to be, the bound alone decides.
No kernel may reach another device: no remote copies, remote signals or barrier semaphores. Data moves between devices by JAX's collectives and lax.ppermute only.
A program may use at most 128 MiB of HBM per device.

```python
import jax
import jax.numpy as jnp
from jax import lax

F = 256
TILE = 128
LAYERS = 2
BLK_DEV = 3
TILES_DEV = 96
CAP = 2
VERTICES = 98304
NTILES = 24576
CBLK = 48
SLOTS = 32
N_GROUP = 16
N_MEMBER = 16


def draw_tile_counts(key, part):
    devices = NTILES // TILES_DEV
    first, second = jax.random.split(jax.random.fold_in(key, 11))
    base = jax.random.randint(first, (devices,), TILES_DEV * 2 // 3, TILES_DEV + 1, dtype=jnp.int32)
    full = jax.random.randint(second, (), 0, devices, dtype=jnp.int32)
    return jnp.where(jnp.arange(devices, dtype=jnp.int32) == full, TILES_DEV, base).astype(jnp.int32)


def draw_mirror_list(key, part):
    devices = NTILES // TILES_DEV
    groups = SLOTS // CAP
    scores = jax.random.randint(jax.random.fold_in(key, 23), (devices, groups, BLK_DEV), 0, 2 ** 20, dtype=jnp.int32)
    scores = scores * BLK_DEV + jnp.arange(BLK_DEV, dtype=jnp.int32)
    order = jnp.argsort(scores, axis=-1, stable=True)
    return order[:, :, :CAP].astype(jnp.int32)


def draw_features(key, part):
    key = jax.random.fold_in(key, 37)
    first, second = jax.random.split(key)
    emphasis = 0.1 * 30.0 ** jax.random.uniform(first, (VERTICES, 8, 1), jnp.float32)
    spread = jax.random.uniform(second, (VERTICES, 8, F // 8), jnp.float32)
    base = 0.1 * 30.0 ** spread
    return (base * emphasis).reshape(VERTICES, F).astype(jnp.float32)


def draw_tiles(key, part):
    key = jax.random.fold_in(key, 41)
    first, second, third = jax.random.split(key, 3)
    row_level = 0.001 * 1000.0 ** jax.random.uniform(first, (NTILES, TILE, 1), jnp.float32)
    col_level = 0.05 * 20.0 ** jax.random.uniform(second, (NTILES, 1, TILE), jnp.float32)
    raw_bits = jax.random.randint(third, (NTILES, TILE, TILE), 0, TILE * 65536, dtype=jnp.int32)
    strong = raw_bits % TILE < 2
    fraction = (raw_bits // TILE).astype(jnp.float32) / 65536.0
    rough = 0.5 + fraction
    level = jnp.where(strong, 1.0, 0.01).astype(jnp.float32)
    return (row_level * col_level * rough * level).astype(jnp.float32)


def touch_ends(entries, key, least, largest):
    spot = [jax.random.randint(jax.random.fold_in(key, axis), (), 0, length) for axis, length in enumerate(entries.shape)]
    main_axis = entries.shape.index(max(entries.shape))
    next_to = spot[:main_axis] + [(spot[main_axis] + 1) % entries.shape[main_axis]] + spot[main_axis + 1:]
    return entries.at[tuple(spot)].set(least).at[tuple(next_to)].set(largest)


def scatter_about(own_key, extent, width, most, kind=jnp.bfloat16):
    return jnp.clip(width * jax.random.normal(own_key, extent, jnp.float32), -most, most).astype(kind)


def setup_inputs(seed: int = 0) -> dict:
    keys = jax.random.split(jax.random.key(seed), 9)
    features = draw_features(jax.random.fold_in(keys[8], 71), 0)
    tiles = draw_tiles(jax.random.fold_in(keys[8], 71), 0)
    tile_col = touch_ends(jax.random.randint(keys[2], (NTILES,), 0, CBLK), jax.random.fold_in(keys[2], 1), 0, CBLK - 1).astype(jnp.int32)
    tile_slot = touch_ends(jax.random.randint(keys[3], (NTILES,), 0, SLOTS), jax.random.fold_in(keys[3], 1), 0, SLOTS - 1).astype(jnp.int32)
    mirror_list = draw_mirror_list(jax.random.fold_in(keys[8], 71), 0)
    tile_counts = draw_tile_counts(jax.random.fold_in(keys[8], 71), 0)
    self_weight = scatter_about(keys[6], (LAYERS, F, F), F ** -0.5, 0.375, jnp.float32)
    neigh_weight = scatter_about(keys[7], (LAYERS, F, F), F ** -0.5, 0.375, jnp.float32)
    return {"features": features, "tiles": tiles, "tile_col": tile_col, "tile_slot": tile_slot, "mirror_list": mirror_list, "tile_counts": tile_counts, "self_weight": self_weight, "neigh_weight": neigh_weight}


def reference(features, tiles, tile_col, tile_slot, mirror_list, tile_counts, self_weight, neigh_weight):
    groups = N_GROUP
    members = N_MEMBER
    devices = groups * members
    tiles_grid = tiles.reshape(devices, TILES_DEV, TILE, TILE)
    col_grid = tile_col.reshape(devices, TILES_DEV)
    slot_grid = tile_slot.reshape(devices, TILES_DEV)
    positions = jnp.arange(TILES_DEV, dtype=jnp.int32)
    targets_all = jnp.arange(groups * BLK_DEV, dtype=jnp.int32)

    def aggregate(state):
        state_grid = state.reshape(groups, members * BLK_DEV, TILE, F)

        def step(carry, item):
            total, degree = carry
            index, block_tiles, cols, slots, mirror, count = item
            grp = index // members
            mem = index % members
            source = lax.dynamic_index_in_dim(state_grid, grp, 0, keepdims=False)
            picked = jnp.take(source, cols, axis=0)
            prods = jnp.einsum('tij,tjf->tif', block_tiles, picked, precision=lax.Precision.HIGHEST)
            live = (positions < count).astype(jnp.float32)
            dest_group = slots // CAP
            target = dest_group * BLK_DEV + mirror[dest_group, slots % CAP]
            onehot = (target[None, :] == targets_all[:, None]).astype(jnp.float32) * live[None, :]
            part = jnp.einsum('nt,tif->nif', onehot, prods, precision=lax.Precision.HIGHEST)
            dpart = jnp.dot(onehot, lax.optimization_barrier(jnp.sum(block_tiles, axis=2)), precision=lax.Precision.HIGHEST)
            part = part.reshape(groups, 1, BLK_DEV, TILE, F)
            dpart = dpart.reshape(groups, 1, BLK_DEV, TILE)
            old = lax.dynamic_slice_in_dim(total, mem, 1, 1)
            total = lax.dynamic_update_slice_in_dim(total, old + part, mem, 1)
            old_deg = lax.dynamic_slice_in_dim(degree, mem, 1, 1)
            degree = lax.dynamic_update_slice_in_dim(degree, old_deg + dpart, mem, 1)
            return ((total, degree), None)
        start = (jnp.zeros((groups, members, BLK_DEV, TILE, F), jnp.float32), jnp.zeros((groups, members, BLK_DEV, TILE), jnp.float32))
        items = (jnp.arange(devices, dtype=jnp.int32), tiles_grid, col_grid, slot_grid, mirror_list, tile_counts)
        (total, degree), _ = lax.scan(step, start, items)
        return (total.reshape(VERTICES, F), degree.reshape(VERTICES))
    state = features
    for layer in range(LAYERS):
        summed, degree = aggregate(state)
        neighbour_mean = (state + summed) / (1.0 + degree)[:, None]
        activated = jax.nn.relu(jnp.dot(state, self_weight[layer], precision=lax.Precision.HIGHEST) + jnp.dot(neighbour_mean, neigh_weight[layer], precision=lax.Precision.HIGHEST))
        state = activated * lax.rsqrt(lax.optimization_barrier(jnp.mean(activated * activated, axis=1, keepdims=True)) + 1e-05)
    return state
```

```python
import functools

import jax
import jax.numpy as jnp
from jax import lax
from jax.experimental import pallas as pl
from jax.experimental.pallas import tpu as pltpu
from jax.sharding import Mesh
from jax.sharding import PartitionSpec as P

F = 256
TILE = 128
LAYERS = 2
BLK_DEV = 3
TILES_DEV = 96
CAP = 2
NZ, NC, NX, NY = 8, 2, 4, 4
AXES = ("z", "c", "x", "y")
UNROLL = 4
SLOTS = TILES_DEV + 4 * UNROLL
ROWS = BLK_DEV * TILE
BF = jnp.bfloat16
F32 = jnp.float32
VMEM = pl.BlockSpec(memory_space=pltpu.VMEM)
SMEM = pl.BlockSpec(memory_space=pltpu.SMEM)


def perm(step):
    pairs = []
    for z in range(NZ):
        for c in range(NC):
            for x in range(NX):
                for y in range(NY):
                    tz, tc, tx, ty = step(z, c, x, y)
                    pairs.append((
                        ((z * NC + c) * NX + x) * NY + y,
                        (((tz % NZ) * NC + tc % NC) * NX + tx % NX) * NY + ty % NY,
                    ))
    return pairs


PAIR = perm(lambda z, c, x, y: (z, c + 1, x, y))


def along_z(d):
    return perm(lambda z, c, x, y: (z + (d if c == 0 else -d), c, x, y))


def in_plane(d, phase):
    return perm(lambda z, c, x, y: (z, c, x + d, y) if (c + phase) % 2 == 0 else (z, c, x, y + d))


def send(value, pairs):
    return lax.ppermute(value, AXES, pairs)


def split(value):
    high = value.astype(BF)
    return high, (value - high.astype(F32)).astype(BF)


def slot_of(offset):
    return jnp.where(offset == 0, 0, jnp.where(offset == 3, 1, jnp.where(offset == 1, 2, 3)))


def late_piece(r):
    return jnp.where(
        r == 3, 0, jnp.where(r == 6, 1, jnp.where(r == 2, 2, jnp.where(r == 7, 3, jnp.where(r == 1, 4, 5))))
    )


def prepare_kernel(place, col, slot, mirror, count, tiles, source, dest, bounds, order, split_tiles, degree, cls, dst, nxt):
    z, c, p, q = place[0], place[1], place[2], place[3]
    for s in range(4):
        nxt[s] = 0

    def classify(t, _):
        sl = slot[t]
        g = sl // CAP
        k = mirror[sl]
        gz, gc = g // NC, g % NC
        r = lax.rem(jnp.where(gc == 0, gz - z, z - gz) + NZ, NZ)
        kept = (gc == c).astype(jnp.int32)
        early = jnp.logical_or(r == 4, r == 5)
        seg = jnp.where(early, 0, 2) + kept
        piece = jnp.where(early, r - 4, late_piece(r))
        live = t < count[0]
        seg = jnp.where(live, seg, 4)
        cls[t] = seg
        dst[t] = piece * 4 + k

        @pl.when(live)
        def _():
            nxt[seg] = nxt[seg] + 1

        return 0

    lax.fori_loop(0, TILES_DEV, classify, 0)
    start = jnp.int32(0)
    for s in range(4):
        chunks = (nxt[s] + UNROLL - 1) // UNROLL
        bounds[s] = start // UNROLL
        nxt[s] = start
        start = start + chunks * UNROLL
    bounds[4] = start // UNROLL

    def clear(s, _):
        order[s] = TILES_DEV
        source[s] = 0
        dest[s] = 0
        return 0

    lax.fori_loop(0, SLOTS, clear, 0)

    def place_tile(t, _):
        seg = cls[t]

        @pl.when(seg < 4)
        def _():
            at = nxt[seg]
            nxt[seg] = at + 1
            b = col[t]
            m, j = b // BLK_DEV, b % BLK_DEV
            bx, by = m // NY, m % NY
            bp = jnp.where(c == 0, bx, by)
            bq = jnp.where(c == 0, by, bx)
            sp = slot_of(lax.rem(bp - p + 4, 4))
            sq = slot_of(lax.rem(bq - q + 4, 4))
            order[at] = t
            source[at] = sq * 12 + sp * 3 + j
            dest[at] = dst[t]

        return 0

    lax.fori_loop(0, TILES_DEV, place_tile, 0)
    degree[...] = jnp.zeros_like(degree)
    ones = jnp.ones((8, TILE), BF)

    def chunk(i, _):
        for u in range(UNROLL):
            s = i * UNROLL + u
            t = order[s]
            live = (t < TILES_DEV).astype(F32)
            high, low = split(tiles[jnp.minimum(t, TILES_DEV - 1)] * live)
            split_tiles[s, :, 0:TILE] = high
            split_tiles[s, :, TILE : 2 * TILE] = low
            nt = (((1,), (1,)), ((), ()))
            row = lax.dot_general(ones, high, nt, preferred_element_type=F32) + lax.dot_general(
                ones, low, nt, preferred_element_type=F32
            )
            seg = (
                (i >= bounds[1]).astype(jnp.int32)
                + (i >= bounds[2]).astype(jnp.int32)
                + (i >= bounds[3]).astype(jnp.int32)
            )
            d = dest[s]
            piece, k = d // 4, d % 4
            at = piece + jnp.where(seg == 0, 0, jnp.where(seg == 1, 2, jnp.where(seg == 2, 4, 10)))
            degree[at, pl.ds(k, 1), :] += row[0:1]
        return 0

    lax.fori_loop(0, bounds[4], chunk, 0)


def prepare(place, col, slot, mirror, count, tiles):
    return pl.pallas_call(
        prepare_kernel,
        out_shape=(
            jax.ShapeDtypeStruct((SLOTS,), jnp.int32),
            jax.ShapeDtypeStruct((SLOTS,), jnp.int32),
            jax.ShapeDtypeStruct((8,), jnp.int32),
            jax.ShapeDtypeStruct((SLOTS,), jnp.int32),
            jax.ShapeDtypeStruct((SLOTS, TILE, 2 * TILE), BF),
            jax.ShapeDtypeStruct((16, 8, TILE), F32),
        ),
        in_specs=[SMEM] * 5 + [VMEM],
        out_specs=(SMEM, SMEM, SMEM, SMEM, VMEM, VMEM),
        scratch_shapes=[
            pltpu.SMEM((TILES_DEV,), jnp.int32),
            pltpu.SMEM((TILES_DEV,), jnp.int32),
            pltpu.SMEM((8,), jnp.int32),
        ],
        compiler_params=pltpu.CompilerParams(vmem_limit_bytes=20 << 20),
        cost_estimate=pl.CostEstimate(flops=10**8, bytes_accessed=13 * 10**6, transcendentals=0),
        name="prepare",
    )(place, col, slot, mirror, count, tiles)


def product_kernel(first, n, rows, source, dest, bounds, degree, tiles, *refs):
    gathered, (sent, kept), (high, low) = refs[:5], refs[5:7], refs[7:]
    base = 0
    for ref in gathered:
        blocks = ref.shape[0] // TILE

        def load(i, _, ref=ref, base=base):
            high[base + i], low[base + i] = split(ref[pl.ds(pl.multiple_of(i * TILE, TILE), TILE), :])
            return 0

        lax.fori_loop(0, blocks, load, 0)
        base += blocks
    for part, out in enumerate((sent, kept)):
        out[...] = jnp.zeros_like(out)
        if rows > ROWS:
            for i in range(n):
                out[i, ROWS:rows, 0:TILE] = degree[(0 if n == 2 else 4) + part * n + i]

        def chunk(i, _, out=out):
            for u in range(UNROLL):
                s = i * UNROLL + u
                b = source[s]
                both = tiles[s]
                value = jnp.dot(
                    jnp.concatenate([both, both[:, :TILE]], axis=1),
                    jnp.concatenate([high[b], high[b], low[b]], axis=0),
                    preferred_element_type=F32,
                )
                d = dest[s]
                piece, k = d // 4, d % 4
                at = pl.ds(pl.multiple_of(k * TILE, TILE), TILE)
                out[piece, at, :] += value
            return 0

        lax.fori_loop(bounds[first + part], bounds[first + part + 1], chunk, 0)


def products(first, n, rows, plan, gathered):
    source, dest, bounds, degree, tiles = plan
    return pl.pallas_call(
        functools.partial(product_kernel, first, n, rows),
        out_shape=(jax.ShapeDtypeStruct((n, rows, F), F32),) * 2,
        in_specs=[SMEM] * 3 + [VMEM] * 7,
        out_specs=(VMEM, VMEM),
        scratch_shapes=[pltpu.VMEM((48, TILE, F), BF)] * 2,
        compiler_params=pltpu.CompilerParams(vmem_limit_bytes=32 << 20),
        cost_estimate=pl.CostEstimate(flops=4 * 10**9 * n // 8, bytes_accessed=15 * 10**6, transcendentals=0),
        name="early" if n == 2 else "late",
    )(source, dest, bounds, degree, tiles, *gathered)


def gather(state):
    a, b, c = (send(state, in_plane(d, 0)) for d in (1, -1, 2))
    own = jnp.concatenate([state, a, b, c], axis=0)
    a, b = send(own, in_plane(1, 1)), send(own, in_plane(-1, 1))
    half = own.shape[0] // 2
    return own, a, b, send(a[:half], in_plane(1, 1)), send(b[half:], in_plane(-1, 1))


def body(features, tiles, tile_col, tile_slot, mirror_list, tile_counts, self_weight, neigh_weight):
    z, c, x, y = (lax.axis_index(a).astype(jnp.int32) for a in AXES)
    place = jnp.stack([z, c, jnp.where(c == 0, x, y), jnp.where(c == 0, y, x)])
    source, dest, bounds, _, split_tiles, degree_part = prepare(
        place, tile_col, tile_slot, mirror_list.reshape(-1), tile_counts, tiles
    )
    plan = (source, dest, bounds, degree_part, split_tiles)
    up, down = along_z(1), along_z(-1)
    state = features
    for layer in range(LAYERS):
        rows = ROWS + 8 if layer == 0 else ROWS
        gathered = gather(state)
        sent, kept = products(0, 2, rows, plan, gathered)
        got = send(sent, PAIR)
        f = send(kept[0] + got[0], up)
        g = send(kept[1] + got[1], down)
        sent, kept = products(2, 6, rows, plan, gathered)
        got = send(sent, PAIR)
        f = send(f + (kept[0] + got[0]), up)
        g = send(g + (kept[1] + got[1]), down)
        f = send(f + (kept[2] + got[2]), up)
        g = send(g + (kept[3] + got[3]), down)
        f = send(f + (kept[4] + got[4]), up)
        total = f + (g + (kept[5] + got[5]))
        if layer == 0:
            degree = total[ROWS : ROWS + BLK_DEV, :TILE].reshape(ROWS)
            total = total[:ROWS]
        neighbour_mean = (state + total) / (1.0 + degree)[:, None]
        activated = jax.nn.relu(
            jnp.dot(state, self_weight[layer], precision=lax.Precision.HIGHEST)
            + jnp.dot(neighbour_mean, neigh_weight[layer], precision=lax.Precision.HIGHEST)
        )
        state = activated * lax.rsqrt(jnp.mean(activated * activated, axis=1, keepdims=True) + 1e-05)
    return state


def solution(mesh):
    fine = Mesh(mesh.devices.reshape(NZ, NC, NX, NY), AXES)
    placed = (
        P(AXES, None),
        P(AXES, None, None),
        P(AXES),
        P(AXES),
        P(AXES, None, None),
        P(AXES),
        P(),
        P(),
    )
    return jax.shard_map(body, mesh=fine, in_specs=placed, out_specs=P(AXES, None), check_vma=False)
```

```python
import functools

import jax
import jax.numpy as jnp
from jax import lax
from jax.experimental import pallas as pl
from jax.experimental.pallas import tpu as pltpu
from jax.sharding import Mesh
from jax.sharding import PartitionSpec as P

F = 256
TILE = 128
LAYERS = 2
BLK_DEV = 3
TILES_DEV = 96
CAP = 2
NZ, NC, NX, NY = 8, 2, 4, 4
AXES = ("z", "c", "x", "y")
UNROLL = 8
SLOTS = TILES_DEV + 4 * UNROLL
ROWS = BLK_DEV * TILE
NT = (((1,), (1,)), ((), ()))
BF = jnp.bfloat16
F32 = jnp.float32
VMEM = pl.BlockSpec(memory_space=pltpu.VMEM)
SMEM = pl.BlockSpec(memory_space=pltpu.SMEM)


def perm(step):
    pairs = []
    for z in range(NZ):
        for c in range(NC):
            for x in range(NX):
                for y in range(NY):
                    tz, tc, tx, ty = step(z, c, x, y)
                    pairs.append((
                        ((z * NC + c) * NX + x) * NY + y,
                        (((tz % NZ) * NC + tc % NC) * NX + tx % NX) * NY + ty % NY,
                    ))
    return pairs


PAIR = perm(lambda z, c, x, y: (z, c + 1, x, y))


def along_z(d):
    return perm(lambda z, c, x, y: (z + (d if c == 0 else -d), c, x, y))


def in_plane(d, phase):
    return perm(lambda z, c, x, y: (z, c, x + d, y) if (c + phase) % 2 == 0 else (z, c, x, y + d))


def send(value, pairs):
    return lax.ppermute(value, AXES, pairs)


def split(value):
    high = value.astype(BF)
    return high, (value - high.astype(F32)).astype(BF)


def slot_of(offset):
    return jnp.where(offset == 0, 0, jnp.where(offset == 3, 1, jnp.where(offset == 1, 2, 3)))


def late_piece(r):
    return jnp.where(
        r == 3, 0, jnp.where(r == 6, 1, jnp.where(r == 2, 2, jnp.where(r == 7, 3, jnp.where(r == 1, 4, 5))))
    )


def plan_kernel(place, col, slot, mirror, count, order, source, dest, bounds, cls, nxt):
    z, c, p, q = place[0], place[1], place[2], place[3]
    for s in range(5):
        nxt[s] = 0
    def classify(t, _):
        sl = slot[t]
        g = sl // CAP
        gz, gc = g // NC, g % NC
        r = lax.bitwise_and(jnp.where(gc == 0, gz - z, z - gz) + NZ, NZ - 1)
        early = jnp.logical_or(r == 4, r == 5)
        seg = jnp.where(early, 0, 2) + (gc == c).astype(jnp.int32)
        seg = jnp.where(t < count[0], seg, 4)
        piece = jnp.where(early, r - 4, late_piece(r))
        cls[t] = seg * 64 + piece * 4 + mirror[sl]
        nxt[seg] = nxt[seg] + 1
        return 0
    lax.fori_loop(0, TILES_DEV, classify, 0)
    start = jnp.int32(0)
    for s in range(4):
        n = nxt[s]
        chunks = (n + UNROLL - 1) // UNROLL
        bounds[s] = start // UNROLL
        nxt[s] = start
        for u in range(UNROLL):
            @pl.when(n > 0)
            def _(start=start,chunks=chunks,u=u):
                at = start + chunks * UNROLL - 1 - u
                order[at] = TILES_DEV
                source[at] = 0
                dest[at] = 0
        start = start + chunks * UNROLL
    bounds[4] = start // UNROLL
    nxt[4] = start
    def place_tile(t, _):
        v = cls[t]
        seg = v // 64
        at = nxt[seg]
        nxt[seg] = at + 1
        b = col[t]
        m = b // BLK_DEV
        j = b - m * BLK_DEV
        bx, by = m // NY, m % NY
        sp = slot_of(lax.bitwise_and(jnp.where(c == 0, bx, by) - p + 4, 3))
        sq = slot_of(lax.bitwise_and(jnp.where(c == 0, by, bx) - q + 4, 3))
        order[at] = t
        source[at] = sq * 12 + sp * 3 + j
        dest[at] = v - seg * 64
        return 0
    lax.fori_loop(0, TILES_DEV, place_tile, 0)
def plan(place, col, slot, mirror, count):
    n = SLOTS + TILES_DEV
    return pl.pallas_call(plan_kernel,
        out_shape=(jax.ShapeDtypeStruct((n,), jnp.int32),)*3+(jax.ShapeDtypeStruct((8,), jnp.int32),),
        in_specs=[SMEM]*5, out_specs=(SMEM,)*4,
        scratch_shapes=[pltpu.SMEM((TILES_DEV,), jnp.int32), pltpu.SMEM((8,), jnp.int32)],
        name="plan")(place, col, slot, mirror, count)


def product_kernel(first, n, rows, order, source, dest, bounds, tiles, *refs):
    gathered, (sent, kept), (high, low) = refs[:8], refs[8:10], refs[10:]
    blocks = gathered[0].shape[0] // TILE
    for i, ref in enumerate(gathered):
        for j in range(blocks):
            high[i * blocks + j], low[i * blocks + j] = split(ref[j * TILE : (j + 1) * TILE, :])
    ones = jnp.ones((8, TILE), BF)
    for part, out in enumerate((sent, kept)):
        out[...] = jnp.zeros_like(out)

        def chunk(i, _, out=out):
            for u in range(UNROLL):
                s = i * UNROLL + u
                b = source[s]
                t = order[s]
                live = (t < TILES_DEV).astype(F32)
                hi, lo = split(tiles[jnp.minimum(t, TILES_DEV - 1)] * live)
                value = jnp.dot(
                    jnp.concatenate([hi, lo, hi], axis=1),
                    jnp.concatenate([high[b], high[b], low[b]], axis=0),
                    preferred_element_type=F32,
                )
                d = dest[s]
                piece, k = d // 4, d % 4
                at = pl.ds(pl.multiple_of(k * TILE, TILE), TILE)
                out[piece, at, :] += value
                if rows > ROWS:
                    row = lax.dot_general(ones, hi, NT, preferred_element_type=F32) + lax.dot_general(
                        ones, lo, NT, preferred_element_type=F32
                    )
                    mine = lax.broadcasted_iota(jnp.int32, (8, TILE), 0) == k
                    out[piece, ROWS:rows, 0:TILE] += jnp.where(mine, row, 0.0)
            return 0

        lax.fori_loop(bounds[first + part], bounds[first + part + 1], chunk, 0)


def products(first, n, rows, plan, tiles, gathered):
    return pl.pallas_call(
        functools.partial(product_kernel, first, n, rows),
        out_shape=(jax.ShapeDtypeStruct((n, rows, F), F32),) * 2,
        in_specs=[SMEM] * 4 + [VMEM] * 9,
        out_specs=(VMEM, VMEM),
        scratch_shapes=[pltpu.VMEM((48, TILE, F), BF)] * 2,
        compiler_params=pltpu.CompilerParams(vmem_limit_bytes=32 << 20),
        cost_estimate=pl.CostEstimate(flops=10**9 * n, bytes_accessed=(6 + n) * 25 * 10**5, transcendentals=0),
        name="early" if n == 2 else "late",
    )(*plan, tiles, *gathered)


def gather(state):
    a, b, c = (send(state, in_plane(d, 0)) for d in (1, -1, 2))
    up, down = in_plane(1, 1), in_plane(-1, 1)
    top, low = jnp.concatenate([state, a], axis=0), jnp.concatenate([b, c], axis=0)
    top_up, top_down = send(top, up), send(top, down)
    low_up, low_down = send(low, up), send(low, down)
    return top, low, top_up, low_up, top_down, low_down, send(top_up, up), send(low_down, down)


def body(features, tiles, tile_col, tile_slot, mirror_list, tile_counts, self_weight, neigh_weight):
    z, c, x, y = (lax.axis_index(a).astype(jnp.int32) for a in AXES)
    place = jnp.stack([z, c, jnp.where(c == 0, x, y), jnp.where(c == 0, y, x)])
    listed = plan(place, tile_col, tile_slot, mirror_list.reshape(-1), tile_counts)
    up, down = along_z(1), along_z(-1)
    state = features
    for layer in range(LAYERS):
        rows = ROWS + 8 if layer == 0 else ROWS
        gathered = gather(state)
        sent, kept = products(0, 2, rows, listed, tiles, gathered)
        got = send(sent, PAIR)
        f = send(kept[0] + got[0], up)
        g = send(kept[1] + got[1], down)
        _, gathered = lax.optimization_barrier((got, gathered))
        sent, kept = products(2, 6, rows, listed, tiles, gathered)
        got = send(sent, PAIR)
        f = send(f + (kept[0] + got[0]), up)
        g = send(g + (kept[1] + got[1]), down)
        f = send(f + (kept[2] + got[2]), up)
        g = send(g + (kept[3] + got[3]), down)
        f = send(f + (kept[4] + got[4]), up)
        total = f + (g + (kept[5] + got[5]))
        if layer == 0:
            degree = total[ROWS : ROWS + BLK_DEV, :TILE].reshape(ROWS)
            total = total[:ROWS]
        neighbour_mean = (state + total) / (1.0 + degree)[:, None]
        activated = jax.nn.relu(
            jnp.dot(state, self_weight[layer], precision=lax.Precision.HIGHEST)
            + jnp.dot(neighbour_mean, neigh_weight[layer], precision=lax.Precision.HIGHEST)
        )
        state = activated * lax.rsqrt(jnp.mean(activated * activated, axis=1, keepdims=True) + 1e-05)
    return state


def solution(mesh):
    fine = Mesh(mesh.devices.reshape(NZ, NC, NX, NY), AXES)
    placed = (
        P(AXES, None),
        P(AXES, None, None),
        P(AXES),
        P(AXES),
        P(AXES, None, None),
        P(AXES),
        P(),
        P(),
    )
    return jax.shard_map(body, mesh=fine, in_specs=placed, out_specs=P(AXES, None), check_vma=False)
```

```python
import functools

import jax
import jax.numpy as jnp
from jax import lax
from jax.experimental import pallas as pl
from jax.experimental.pallas import tpu as pltpu
from jax.sharding import Mesh
from jax.sharding import PartitionSpec as P

F = 256
TILE = 128
LAYERS = 2
BLK_DEV = 3
TILES_DEV = 96
CAP = 2
NZ, NC, NX, NY = 8, 2, 4, 4
AXES = ("z", "c", "x", "y")
UNROLL = 8
PIECES = (2, 2, 4)
SEGMENTS = 6
SLOTS = 2 * TILES_DEV + SEGMENTS * UNROLL
SOURCE, DEST, BOUNDS = SLOTS, 2 * SLOTS, 3 * SLOTS
LISTED = 3 * SLOTS + 8
ROWS = BLK_DEV * TILE
NT = (((1,), (1,)), ((), ()))
BF = jnp.bfloat16
F32 = jnp.float32
VMEM = pl.BlockSpec(memory_space=pltpu.VMEM)
SMEM = pl.BlockSpec(memory_space=pltpu.SMEM)


def perm(step):
    pairs = []
    for z in range(NZ):
        for c in range(NC):
            for x in range(NX):
                for y in range(NY):
                    tz, tc, tx, ty = step(z, c, x, y)
                    pairs.append((
                        ((z * NC + c) * NX + x) * NY + y,
                        (((tz % NZ) * NC + tc % NC) * NX + tx % NX) * NY + ty % NY,
                    ))
    return pairs


PAIR = perm(lambda z, c, x, y: (z, c + 1, x, y))


def along_z(d):
    return perm(lambda z, c, x, y: (z + (d if c == 0 else -d), c, x, y))


def in_plane(d, phase):
    return perm(lambda z, c, x, y: (z, c, x + d, y) if (c + phase) % 2 == 0 else (z, c, x, y + d))


def send(value, pairs):
    return lax.ppermute(value, AXES, pairs)


def split(value):
    high = value.astype(BF)
    return high, (value - high.astype(F32)).astype(BF)


def slot_of(offset):
    return jnp.where(offset == 0, 0, jnp.where(offset == 3, 1, jnp.where(offset == 1, 2, 3)))


def piece_of(r):
    return jnp.where(
        r == 3, 0, jnp.where(r == 6, 1, jnp.where(r == 2, 0, jnp.where(r == 7, 1, jnp.where(r == 1, 2, 3))))
    )


def plan_kernel(place, col, slot, mirror, count, listed, cls, nxt):
    z, c, p, q = place[0], place[1], place[2], place[3]
    for s in range(7):
        nxt[s] = 0

    def classify(t, _):
        sl = slot[t]
        g = sl // CAP
        gz, gc = g // NC, g % NC
        r = lax.bitwise_and(jnp.where(gc == 0, gz - z, z - gz) + NZ, NZ - 1)
        first = jnp.logical_or(r == 4, r == 5)
        second = jnp.logical_or(r == 3, r == 6)
        seg = jnp.where(first, 0, jnp.where(second, 2, 4)) + (gc == c).astype(jnp.int32)
        seg = jnp.where(t < count[0], seg, SEGMENTS)
        piece = jnp.where(first, r - 4, piece_of(r))
        cls[t] = seg * 64 + piece * 4 + mirror[sl]
        nxt[seg] = nxt[seg] + 1
        return 0

    lax.fori_loop(0, TILES_DEV, classify, 0)
    start = jnp.int32(0)
    for s in range(SEGMENTS):
        n = nxt[s]
        end = start + (n + UNROLL - 1) // UNROLL * UNROLL
        listed[BOUNDS + s] = start // UNROLL
        nxt[s] = start

        def pad(at, _):
            listed[at] = TILES_DEV
            listed[SOURCE + at] = 0
            listed[DEST + at] = 0
            return 0

        lax.fori_loop(start + n, end, pad, 0)
        start = end
    listed[BOUNDS + SEGMENTS] = start // UNROLL
    nxt[SEGMENTS] = start

    def place_tile(t, _):
        v = cls[t]
        seg = v // 64
        at = nxt[seg]
        nxt[seg] = at + 1
        b = col[t]
        m = b // BLK_DEV
        j = b - m * BLK_DEV
        bx, by = m // NY, m % NY
        sp = slot_of(lax.bitwise_and(jnp.where(c == 0, bx, by) - p + 4, 3))
        sq = slot_of(lax.bitwise_and(jnp.where(c == 0, by, bx) - q + 4, 3))
        listed[at] = t
        listed[SOURCE + at] = sq * 12 + sp * 3 + j
        listed[DEST + at] = v - seg * 64
        return 0

    lax.fori_loop(0, TILES_DEV, place_tile, 0)


def plan(place, col, slot, mirror, count):
    return pl.pallas_call(
        plan_kernel,
        out_shape=jax.ShapeDtypeStruct((LISTED,), jnp.int32),
        in_specs=[SMEM] * 5,
        out_specs=SMEM,
        scratch_shapes=[pltpu.SMEM((TILES_DEV,), jnp.int32), pltpu.SMEM((8,), jnp.int32)],
        cost_estimate=pl.CostEstimate(flops=0, bytes_accessed=2 * 10**7, transcendentals=0),
        name="plan",
    )(place, col, slot, mirror, count)


def tile_at(listed, tiles, s):
    t = listed[s]
    live = (t < TILES_DEV).astype(F32)
    return split(tiles[jnp.minimum(t, TILES_DEV - 1)] * live)


def degree_kernel(listed, tiles, degree):
    degree[...] = jnp.zeros_like(degree)
    ones = jnp.ones((8, TILE), BF)
    base = 0
    for seg in range(SEGMENTS):

        def chunk(i, _, base=base):
            for u in range(UNROLL):
                s = i * UNROLL + u
                hi, lo = tile_at(listed, tiles, s)
                row = lax.dot_general(ones, hi, NT, preferred_element_type=F32) + lax.dot_general(
                    ones, lo, NT, preferred_element_type=F32
                )
                d = listed[DEST + s]
                degree[base + d // 4, pl.ds(d % 4, 1), :] += row[0:1]
            return 0

        lax.fori_loop(listed[BOUNDS + seg], listed[BOUNDS + seg + 1], chunk, 0)
        base += PIECES[seg // 2]


def degrees(listed, tiles):
    return pl.pallas_call(
        degree_kernel,
        out_shape=jax.ShapeDtypeStruct((2 * NZ, 8, TILE), F32),
        in_specs=[SMEM, VMEM],
        out_specs=VMEM,
        compiler_params=pltpu.CompilerParams(vmem_limit_bytes=16 << 20),
        cost_estimate=pl.CostEstimate(flops=10**8, bytes_accessed=2 * 10**7, transcendentals=0),
        name="degrees",
    )(listed, tiles)


def product_kernel(stages, rows, listed, tiles, degree, *refs):
    gathered, outs, (high, low) = refs[:8], refs[8:-2], refs[-2:]
    blocks = gathered[0].shape[0] // TILE
    for i, ref in enumerate(gathered):
        for j in range(blocks):
            high[i * blocks + j], low[i * blocks + j] = split(ref[j * TILE : (j + 1) * TILE, :])
    for seg, out in zip(range(2 * stages.start, 2 * stages.stop), outs):
        out[...] = jnp.zeros_like(out)
        if rows > ROWS:
            n, base = out.shape[0], sum(PIECES[s // 2] for s in range(seg))
            out[:, ROWS:rows, 0:TILE] = degree[base : base + n]

        def chunk(i, _, out=out):
            for u in range(UNROLL):
                s = i * UNROLL + u
                b = listed[SOURCE + s]
                hi, lo = tile_at(listed, tiles, s)
                value = jnp.dot(
                    jnp.concatenate([hi, lo, hi], axis=1),
                    jnp.concatenate([high[b], high[b], low[b]], axis=0),
                    preferred_element_type=F32,
                )
                d = listed[DEST + s]
                at = pl.ds(pl.multiple_of(d % 4 * TILE, TILE), TILE)
                out[d // 4, at, :] += value
            return 0

        lax.fori_loop(listed[BOUNDS + seg], listed[BOUNDS + seg + 1], chunk, 0)


def products(stages, rows, listed, tiles, degree, gathered):
    n = sum(PIECES[s] for s in stages)
    return pl.pallas_call(
        functools.partial(product_kernel, stages, rows),
        out_shape=tuple(jax.ShapeDtypeStruct((PIECES[s], rows, F), F32) for s in stages for _ in range(2)),
        in_specs=[SMEM] + [VMEM] * 10,
        out_specs=(VMEM,) * (2 * len(stages)),
        scratch_shapes=[pltpu.VMEM((48, TILE, F), BF)] * 2,
        compiler_params=pltpu.CompilerParams(vmem_limit_bytes=32 << 20),
        cost_estimate=pl.CostEstimate(flops=10**9 * n, bytes_accessed=(6 + n) * 25 * 10**5, transcendentals=0),
        name="early" if n == 2 else "late",
    )(listed, tiles, degree, *gathered)


def gather(state, meanwhile=None):
    a, b, c = (send(state, in_plane(d, 0)) for d in (1, -1, 2))
    if meanwhile is not None:
        a, meanwhile = lax.optimization_barrier((a, meanwhile))
    up, down = in_plane(1, 1), in_plane(-1, 1)
    top, low = jnp.concatenate([state, a], axis=0), jnp.concatenate([b, c], axis=0)
    top_up, top_down = send(top, up), send(top, down)
    low_up, low_down = send(low, up), send(low, down)
    return (top, low, top_up, low_up, top_down, low_down, send(top_up, up), send(low_down, down)), meanwhile


def body(features, tiles, tile_col, tile_slot, mirror_list, tile_counts, self_weight, neigh_weight):
    z, c, x, y = (lax.axis_index(a).astype(jnp.int32) for a in AXES)
    place = jnp.stack([z, c, jnp.where(c == 0, x, y), jnp.where(c == 0, y, x)])
    listed = plan(place, tile_col, tile_slot, mirror_list.reshape(-1), tile_counts)
    up, down = along_z(1), along_z(-1)
    state = features
    for layer in range(LAYERS):
        rows = ROWS + 8 if layer == 0 else ROWS
        if layer == 0:
            gathered, listed = gather(state, listed)
            degree_part = degrees(listed, tiles)
        else:
            gathered, _ = gather(state)
        sent, kept = products(range(0, 1), rows, listed, tiles, degree_part, gathered)
        got = send(sent, PAIR)
        f, g = kept[0] + got[0], kept[1] + got[1]
        _, gathered = lax.optimization_barrier((got, gathered))
        sent, kept, sent_last, kept_last = products(range(1, 3), rows, listed, tiles, degree_part, gathered)
        f, g = send(f, up), send(g, down)
        f, g, sent, sent_last = lax.optimization_barrier((f, g, sent, sent_last))
        got, got_last = send(sent, PAIR), send(sent_last, PAIR)
        f = send(f + (kept[0] + got[0]), up)
        g = send(g + (kept[1] + got[1]), down)
        f = send(f + (kept_last[0] + got_last[0]), up)
        g = send(g + (kept_last[1] + got_last[1]), down)
        f = send(f + (kept_last[2] + got_last[2]), up)
        total = f + (g + (kept_last[3] + got_last[3]))
        if layer == 0:
            degree = total[ROWS : ROWS + BLK_DEV, :TILE].reshape(ROWS)
            total = total[:ROWS]
        neighbour_mean = (state + total) / (1.0 + degree)[:, None]
        activated = jax.nn.relu(
            jnp.dot(state, self_weight[layer], precision=lax.Precision.HIGHEST)
            + jnp.dot(neighbour_mean, neigh_weight[layer], precision=lax.Precision.HIGHEST)
        )
        state = activated * lax.rsqrt(jnp.mean(activated * activated, axis=1, keepdims=True) + 1e-05)
    return state


def solution(mesh):
    fine = Mesh(mesh.devices.reshape(NZ, NC, NX, NY), AXES)
    placed = (
        P(AXES, None),
        P(AXES, None, None),
        P(AXES),
        P(AXES),
        P(AXES, None, None),
        P(AXES),
        P(),
        P(),
    )
    return jax.shard_map(body, mesh=fine, in_specs=placed, out_specs=P(AXES, None), check_vma=False)
```

```python
import functools

import jax
import jax.numpy as jnp
from jax import lax
from jax.experimental import pallas as pl
from jax.experimental.pallas import tpu as pltpu
from jax.sharding import Mesh
from jax.sharding import PartitionSpec as P

F = 256
TILE = 128
LAYERS = 2
BLK_DEV = 3
TILES_DEV = 96
CAP = 2
NZ, NC, NX, NY = 8, 2, 4, 4
AXES = ("z", "c", "x", "y")
UNROLL = 8
PIECES = (2, 2, 4)
SEGMENTS = 6
SLOTS = 2 * TILES_DEV + SEGMENTS * UNROLL
SOURCE, DEST, BOUNDS = SLOTS, 2 * SLOTS, 3 * SLOTS
LISTED = 3 * SLOTS + 8
ROWS = BLK_DEV * TILE
NT = (((1,), (1,)), ((), ()))
BF = jnp.bfloat16
F32 = jnp.float32
VMEM = pl.BlockSpec(memory_space=pltpu.VMEM)
SMEM = pl.BlockSpec(memory_space=pltpu.SMEM)


def perm(step):
    pairs = []
    for z in range(NZ):
        for c in range(NC):
            for x in range(NX):
                for y in range(NY):
                    tz, tc, tx, ty = step(z, c, x, y)
                    pairs.append((
                        ((z * NC + c) * NX + x) * NY + y,
                        (((tz % NZ) * NC + tc % NC) * NX + tx % NX) * NY + ty % NY,
                    ))
    return pairs


PAIR = perm(lambda z, c, x, y: (z, c + 1, x, y))


def along_z(d):
    return perm(lambda z, c, x, y: (z + (d if c == 0 else -d), c, x, y))


def in_plane(d, phase):
    return perm(lambda z, c, x, y: (z, c, x + d, y) if (c + phase) % 2 == 0 else (z, c, x, y + d))


def send(value, pairs):
    return lax.ppermute(value, AXES, pairs)


def split(value):
    high = value.astype(BF)
    return high, (value - high.astype(F32)).astype(BF)


def slot_of(offset):
    return jnp.where(offset == 0, 0, jnp.where(offset == 3, 1, jnp.where(offset == 1, 2, 3)))


def piece_of(r):
    return jnp.where(
        r == 3, 0, jnp.where(r == 6, 1, jnp.where(r == 2, 0, jnp.where(r == 7, 1, jnp.where(r == 1, 2, 3))))
    )


def plan_kernel(place, col, slot, mirror, count, listed, cls, nxt):
    z, c, p, q = place[0], place[1], place[2], place[3]
    for s in range(7):
        nxt[s] = 0

    def classify(t, _):
        sl = slot[t]
        g = sl // CAP
        gz, gc = g // NC, g % NC
        r = lax.bitwise_and(jnp.where(gc == 0, gz - z, z - gz) + NZ, NZ - 1)
        first = jnp.logical_or(r == 4, r == 5)
        second = jnp.logical_or(r == 3, r == 6)
        seg = jnp.where(first, 0, jnp.where(second, 2, 4)) + (gc == c).astype(jnp.int32)
        seg = jnp.where(t < count[0], seg, SEGMENTS)
        piece = jnp.where(first, r - 4, piece_of(r))
        cls[t] = seg * 64 + piece * 4 + mirror[sl]
        nxt[seg] = nxt[seg] + 1
        return 0

    lax.fori_loop(0, TILES_DEV, classify, 0)
    start = jnp.int32(0)
    for s in range(SEGMENTS):
        n = nxt[s]
        end = start + (n + UNROLL - 1) // UNROLL * UNROLL
        listed[BOUNDS + s] = start // UNROLL
        nxt[s] = start

        def pad(at, _):
            listed[at] = TILES_DEV
            listed[SOURCE + at] = 0
            listed[DEST + at] = 0
            return 0

        lax.fori_loop(start + n, end, pad, 0)
        start = end
    listed[BOUNDS + SEGMENTS] = start // UNROLL
    nxt[SEGMENTS] = start

    def place_tile(t, _):
        v = cls[t]
        seg = v // 64
        at = nxt[seg]
        nxt[seg] = at + 1
        b = col[t]
        m = b // BLK_DEV
        j = b - m * BLK_DEV
        bx, by = m // NY, m % NY
        sp = slot_of(lax.bitwise_and(jnp.where(c == 0, bx, by) - p + 4, 3))
        sq = slot_of(lax.bitwise_and(jnp.where(c == 0, by, bx) - q + 4, 3))
        listed[at] = t
        listed[SOURCE + at] = sq * 12 + sp * 3 + j
        listed[DEST + at] = v - seg * 64
        return 0

    lax.fori_loop(0, TILES_DEV, place_tile, 0)


def plan(place, col, slot, mirror, count):
    return pl.pallas_call(
        plan_kernel,
        out_shape=jax.ShapeDtypeStruct((LISTED,), jnp.int32),
        in_specs=[SMEM] * 5,
        out_specs=SMEM,
        scratch_shapes=[pltpu.SMEM((TILES_DEV,), jnp.int32), pltpu.SMEM((8,), jnp.int32)],
        cost_estimate=pl.CostEstimate(flops=0, bytes_accessed=2 * 10**7, transcendentals=0),
        name="plan",
    )(place, col, slot, mirror, count)


def tile_at(listed, tiles, s):
    t = listed[s]
    live = (t < TILES_DEV).astype(F32)
    return split(tiles[jnp.minimum(t, TILES_DEV - 1)] * live)


def degree_kernel(listed, tiles, degree):
    degree[...] = jnp.zeros_like(degree)
    ones = jnp.ones((8, TILE), BF)
    base = 0
    for seg in range(SEGMENTS):

        def chunk(i, _, base=base):
            for u in range(UNROLL):
                s = i * UNROLL + u
                hi, lo = tile_at(listed, tiles, s)
                row = lax.dot_general(ones, hi, NT, preferred_element_type=F32) + lax.dot_general(
                    ones, lo, NT, preferred_element_type=F32
                )
                d = listed[DEST + s]
                degree[base + d // 4, pl.ds(d % 4, 1), :] += row[0:1]
            return 0

        lax.fori_loop(listed[BOUNDS + seg], listed[BOUNDS + seg + 1], chunk, 0)
        base += PIECES[seg // 2]


def degrees(listed, tiles):
    return pl.pallas_call(
        degree_kernel,
        out_shape=jax.ShapeDtypeStruct((2 * NZ, 8, TILE), F32),
        in_specs=[SMEM, VMEM],
        out_specs=VMEM,
        compiler_params=pltpu.CompilerParams(vmem_limit_bytes=16 << 20),
        cost_estimate=pl.CostEstimate(flops=10**8, bytes_accessed=2 * 10**7, transcendentals=0),
        name="degrees",
    )(listed, tiles)


def add_products(stage, rows, listed, tiles, degree, high, low, outs):
    for part, out in enumerate(outs):
        seg = 2 * stage + part
        out[...] = jnp.zeros_like(out)
        if rows > ROWS:
            n, base = out.shape[0], sum(PIECES[s // 2] for s in range(seg))
            out[:, ROWS:rows, 0:TILE] = degree[base : base + n]

        def chunk(i, _, out=out):
            for u in range(UNROLL):
                s = i * UNROLL + u
                b = listed[SOURCE + s]
                hi, lo = tile_at(listed, tiles, s)
                value = jnp.dot(
                    jnp.concatenate([hi, lo, hi], axis=1),
                    jnp.concatenate([high[b], high[b], low[b]], axis=0),
                    preferred_element_type=F32,
                )
                d = listed[DEST + s]
                at = pl.ds(pl.multiple_of(d % 4 * TILE, TILE), TILE)
                out[d // 4, at, :] += value
            return 0

        lax.fori_loop(listed[BOUNDS + seg], listed[BOUNDS + seg + 1], chunk, 0)


def first_kernel(rows, listed, tiles, degree, *refs):
    gathered, (sent, kept, high, low) = refs[:8], refs[8:]
    blocks = gathered[0].shape[0] // TILE
    for i, ref in enumerate(gathered):
        for j in range(blocks):
            high[i * blocks + j], low[i * blocks + j] = split(ref[j * TILE : (j + 1) * TILE, :])
    add_products(0, rows, listed, tiles, degree, high, low, (sent, kept))


def next_kernel(stage, rows, listed, tiles, degree, high, low, sent, kept):
    add_products(stage, rows, listed, tiles, degree, high, low, (sent, kept))


def products(stage, rows, listed, tiles, degree, sources):
    n = PIECES[stage]
    outs = [jax.ShapeDtypeStruct((n, rows, F), F32)] * 2
    if stage == 0:
        kernel = functools.partial(first_kernel, rows)
        outs += [jax.ShapeDtypeStruct((48, TILE, F), BF)] * 2
    else:
        kernel = functools.partial(next_kernel, stage, rows)
    return pl.pallas_call(
        kernel,
        out_shape=tuple(outs),
        in_specs=[SMEM] + [VMEM] * (2 + len(sources)),
        out_specs=(VMEM,) * len(outs),
        compiler_params=pltpu.CompilerParams(vmem_limit_bytes=32 << 20),
        cost_estimate=pl.CostEstimate(flops=10**9 * n, bytes_accessed=n * 40 * 10**5, transcendentals=0),
        name=("early", "mid", "late")[stage],
    )(listed, tiles, degree, *sources)


def gather(state, meanwhile=None):
    a, b, c = (send(state, in_plane(d, 0)) for d in (1, -1, 2))
    a, b, c, meanwhile = lax.optimization_barrier((a, b, c, meanwhile))
    up, down = in_plane(1, 1), in_plane(-1, 1)
    top, low = jnp.concatenate([state, a], axis=0), jnp.concatenate([b, c], axis=0)
    top, low = lax.optimization_barrier((top, low))
    top_up, top_down = send(top, up), send(top, down)
    low_up, low_down = send(low, up), send(low, down)
    return (top, low, top_up, low_up, top_down, low_down, send(top_up, up), send(low_down, down)), meanwhile


def body(features, tiles, tile_col, tile_slot, mirror_list, tile_counts, self_weight, neigh_weight):
    z, c, x, y = (lax.axis_index(a).astype(jnp.int32) for a in AXES)
    place = jnp.stack([z, c, jnp.where(c == 0, x, y), jnp.where(c == 0, y, x)])
    listed = plan(place, tile_col, tile_slot, mirror_list.reshape(-1), tile_counts)
    up, down = along_z(1), along_z(-1)
    state = features
    for layer in range(LAYERS):
        rows = ROWS + 8 if layer == 0 else ROWS
        if layer == 0:
            gathered, listed = gather(state, listed)
            degree_part = degrees(listed, tiles)
        else:
            gathered, _ = gather(state)
        sent, kept, high, low = products(0, rows, listed, tiles, degree_part, gathered)
        got = send(sent, PAIR)
        sent_mid, kept_mid = products(1, rows, listed, tiles, degree_part, (high, low))
        got, sent_mid, high, low = lax.optimization_barrier((got, sent_mid, high, low))
        got_mid = send(sent_mid, PAIR)
        f, g = send(kept[0] + got[0], up), send(kept[1] + got[1], down)
        sent_last, kept_last = products(2, rows, listed, tiles, degree_part, (high, low))
        f, g, got_mid, sent_last = lax.optimization_barrier((f, g, got_mid, sent_last))
        got_last = send(sent_last, PAIR)
        f = send(f + (kept_mid[0] + got_mid[0]), up)
        g = send(g + (kept_mid[1] + got_mid[1]), down)
        f = send(f + (kept_last[0] + got_last[0]), up)
        g = send(g + (kept_last[1] + got_last[1]), down)
        f = send(f + (kept_last[2] + got_last[2]), up)
        total = f + (g + (kept_last[3] + got_last[3]))
        if layer == 0:
            degree = total[ROWS : ROWS + BLK_DEV, :TILE].reshape(ROWS)
            total = total[:ROWS]
        neighbour_mean = (state + total) / (1.0 + degree)[:, None]
        activated = jax.nn.relu(
            jnp.dot(state, self_weight[layer], precision=lax.Precision.HIGHEST)
            + jnp.dot(neighbour_mean, neigh_weight[layer], precision=lax.Precision.HIGHEST)
        )
        state = activated * lax.rsqrt(jnp.mean(activated * activated, axis=1, keepdims=True) + 1e-05)
    return state


def solution(mesh):
    fine = Mesh(mesh.devices.reshape(NZ, NC, NX, NY), AXES)
    placed = (
        P(AXES, None),
        P(AXES, None, None),
        P(AXES),
        P(AXES),
        P(AXES, None, None),
        P(AXES),
        P(),
        P(),
    )
    return jax.shard_map(body, mesh=fine, in_specs=placed, out_specs=P(AXES, None), check_vma=False)
```

```python
import functools

import jax
import jax.numpy as jnp
from jax import lax
from jax.experimental import pallas as pl
from jax.experimental.pallas import tpu as pltpu
from jax.sharding import Mesh
from jax.sharding import PartitionSpec as P

F = 256
TILE = 128
LAYERS = 2
BLK_DEV = 3
TILES_DEV = 96
CAP = 2
NZ, NC, NX, NY = 8, 2, 4, 4
AXES = ("z", "c", "x", "y")
UNROLL = 8
PIECES = (2, 2, 4)
BASE = (0, 4, 8)
SEGMENTS = len(PIECES)
SLOTS = 2 * TILES_DEV + SEGMENTS * UNROLL
SOURCE, DEST, BOUNDS = SLOTS, 2 * SLOTS, 3 * SLOTS
LISTED = 3 * SLOTS + 8
ROWS = BLK_DEV * TILE
NT = (((1,), (1,)), ((), ()))
BF = jnp.bfloat16
F32 = jnp.float32
VMEM = pl.BlockSpec(memory_space=pltpu.VMEM)
SMEM = pl.BlockSpec(memory_space=pltpu.SMEM)


def perm(step):
    pairs = []
    for z in range(NZ):
        for c in range(NC):
            for x in range(NX):
                for y in range(NY):
                    tz, tc, tx, ty = step(z, c, x, y)
                    pairs.append((
                        ((z * NC + c) * NX + x) * NY + y,
                        (((tz % NZ) * NC + tc % NC) * NX + tx % NX) * NY + ty % NY,
                    ))
    return pairs


PAIR = perm(lambda z, c, x, y: (z, c + 1, x, y))


def along_z(d):
    return perm(lambda z, c, x, y: (z + (d if c == 0 else -d), c, x, y))


def in_plane(d, phase):
    return perm(lambda z, c, x, y: (z, c, x + d, y) if (c + phase) % 2 == 0 else (z, c, x, y + d))


def send(value, pairs):
    return lax.ppermute(value, AXES, pairs)


def split(value):
    high = value.astype(BF)
    return high, (value - high.astype(F32)).astype(BF)


def slot_of(offset):
    return jnp.where(offset == 0, 0, jnp.where(offset == 3, 1, jnp.where(offset == 1, 2, 3)))


def piece_of(r):
    return jnp.where(
        r == 3, 0, jnp.where(r == 6, 1, jnp.where(r == 2, 0, jnp.where(r == 7, 1, jnp.where(r == 1, 2, 3))))
    )


def plan_kernel(place, col, slot, mirror, count, listed, cls, nxt):
    z, c, p, q = place[0], place[1], place[2], place[3]
    for s in range(SEGMENTS + 1):
        nxt[s] = 0

    def classify(t, _):
        sl = slot[t]
        g = sl // CAP
        gz, gc = g // NC, g % NC
        r = lax.bitwise_and(jnp.where(gc == 0, gz - z, z - gz) + NZ, NZ - 1)
        first = jnp.logical_or(r == 4, r == 5)
        second = jnp.logical_or(r == 3, r == 6)
        seg = jnp.where(first, 0, jnp.where(second, 1, 2))
        piece = jnp.where(first, r - 4, piece_of(r)) + BASE[1] * seg
        piece += jnp.where(gc == c, jnp.where(seg == 2, PIECES[2], PIECES[0]), 0)
        seg = jnp.where(t < count[0], seg, SEGMENTS)
        cls[t] = seg * 64 + piece * 4 + mirror[sl]
        nxt[seg] = nxt[seg] + 1
        return 0

    lax.fori_loop(0, TILES_DEV, classify, 0)
    start = jnp.int32(0)
    for s in range(SEGMENTS):
        n = nxt[s]
        end = start + (n + UNROLL - 1) // UNROLL * UNROLL
        listed[BOUNDS + s] = start // UNROLL
        nxt[s] = start

        def pad(at, _):
            listed[at] = TILES_DEV
            listed[SOURCE + at] = 0
            listed[DEST + at] = 0
            return 0

        lax.fori_loop(start + n, end, pad, 0)
        start = end
    listed[BOUNDS + SEGMENTS] = start // UNROLL
    nxt[SEGMENTS] = start

    def place_tile(t, _):
        v = cls[t]
        seg = v // 64
        at = nxt[seg]
        nxt[seg] = at + 1
        b = col[t]
        m = b // BLK_DEV
        j = b - m * BLK_DEV
        bx, by = m // NY, m % NY
        sp = slot_of(lax.bitwise_and(jnp.where(c == 0, bx, by) - p + 4, 3))
        sq = slot_of(lax.bitwise_and(jnp.where(c == 0, by, bx) - q + 4, 3))
        listed[at] = t
        listed[SOURCE + at] = sq * 12 + sp * 3 + j
        listed[DEST + at] = v - seg * 64
        return 0

    lax.fori_loop(0, TILES_DEV, place_tile, 0)


def plan(place, col, slot, mirror, count):
    return pl.pallas_call(
        plan_kernel,
        out_shape=jax.ShapeDtypeStruct((LISTED,), jnp.int32),
        in_specs=[SMEM] * 5,
        out_specs=SMEM,
        scratch_shapes=[pltpu.SMEM((TILES_DEV,), jnp.int32), pltpu.SMEM((8,), jnp.int32)],
        cost_estimate=pl.CostEstimate(flops=0, bytes_accessed=2 * 10**7, transcendentals=0),
        name="plan",
    )(place, col, slot, mirror, count)


def tile_at(listed, tiles, s):
    t = listed[s]
    live = (t < TILES_DEV).astype(F32)
    return split(tiles[jnp.minimum(t, TILES_DEV - 1)] * live)


def degree_kernel(listed, tiles, degree):
    degree[...] = jnp.zeros_like(degree)
    ones = jnp.ones((8, TILE), BF)

    def chunk(i, _):
        for u in range(UNROLL):
            s = i * UNROLL + u
            hi, lo = tile_at(listed, tiles, s)
            row = lax.dot_general(ones, hi, NT, preferred_element_type=F32) + lax.dot_general(
                ones, lo, NT, preferred_element_type=F32
            )
            d = listed[DEST + s]
            degree[d // 4, pl.ds(d % 4, 1), :] += row[0:1]
        return 0

    lax.fori_loop(0, listed[BOUNDS + SEGMENTS], chunk, 0)


def degrees(listed, tiles):
    return pl.pallas_call(
        degree_kernel,
        out_shape=jax.ShapeDtypeStruct((2 * NZ, 8, TILE), F32),
        in_specs=[SMEM, VMEM],
        out_specs=VMEM,
        compiler_params=pltpu.CompilerParams(vmem_limit_bytes=16 << 20),
        cost_estimate=pl.CostEstimate(flops=10**8, bytes_accessed=2 * 10**7, transcendentals=0),
        name="degrees",
    )(listed, tiles)


def add_products(stage, rows, listed, tiles, degree, high, low, out):
    places, base = out.shape[0], BASE[stage]

    def clear(i, _):
        out[i] = jnp.zeros((rows, F), F32)
        if rows > ROWS:
            out[i, ROWS:rows, 0:TILE] = degree[base + i]
        return 0

    lax.fori_loop(0, places, clear, 0)

    def chunk(i, _):
        for u in range(UNROLL):
            s = i * UNROLL + u
            b = listed[SOURCE + s]
            hi, lo = tile_at(listed, tiles, s)
            value = jnp.dot(
                jnp.concatenate([hi, lo, hi], axis=1),
                jnp.concatenate([high[b], high[b], low[b]], axis=0),
                preferred_element_type=F32,
            )
            d = listed[DEST + s]
            at = pl.ds(pl.multiple_of(d % 4 * TILE, TILE), TILE)
            out[jnp.maximum(d // 4 - base, 0), at, :] += value
        return 0

    lax.fori_loop(listed[BOUNDS + stage], listed[BOUNDS + stage + 1], chunk, 0)


def first_kernel(rows, listed, tiles, degree, *refs):
    gathered, (out, high, low) = refs[:8], refs[8:]
    blocks = gathered[0].shape[0] // TILE
    for i, ref in enumerate(gathered):

        def load(j, _, i=i, ref=ref):
            at = pl.ds(pl.multiple_of(j * TILE, TILE), TILE)
            high[i * blocks + j], low[i * blocks + j] = split(ref[at, :])
            return 0

        lax.fori_loop(0, blocks, load, 0)
    add_products(0, rows, listed, tiles, degree, high, low, out)


def next_kernel(stage, rows, listed, tiles, degree, high, low, out):
    add_products(stage, rows, listed, tiles, degree, high, low, out)


def products(stage, rows, listed, tiles, degree, sources):
    n = PIECES[stage]
    outs = [jax.ShapeDtypeStruct((2 * n, rows, F), F32)]
    if stage == 0:
        kernel = functools.partial(first_kernel, rows)
        outs += [jax.ShapeDtypeStruct((48, TILE, F), BF)] * 2
    else:
        kernel = functools.partial(next_kernel, stage, rows)
    out, *halves = pl.pallas_call(
        kernel,
        out_shape=tuple(outs),
        in_specs=[SMEM] + [VMEM] * (2 + len(sources)),
        out_specs=(VMEM,) * len(outs),
        compiler_params=pltpu.CompilerParams(vmem_limit_bytes=32 << 20),
        cost_estimate=pl.CostEstimate(flops=10**9 * n, bytes_accessed=n * 40 * 10**5, transcendentals=0),
        name=("early", "mid", "late")[stage],
    )(listed, tiles, degree, *sources)
    return out[:n], out[n:], *halves


def gather(state, meanwhile=None):
    a, b, c = (send(state, in_plane(d, 0)) for d in (1, -1, 2))
    a, b, c, meanwhile = lax.optimization_barrier((a, b, c, meanwhile))
    up, down = in_plane(1, 1), in_plane(-1, 1)
    top, low = jnp.concatenate([state, a], axis=0), jnp.concatenate([b, c], axis=0)
    top, low = lax.optimization_barrier((top, low))
    top_up, top_down = send(top, up), send(top, down)
    low_up, low_down = send(low, up), send(low, down)
    return (top, low, top_up, low_up, top_down, low_down, send(top_up, up), send(low_down, down)), meanwhile


def body(features, tiles, tile_col, tile_slot, mirror_list, tile_counts, self_weight, neigh_weight):
    z, c, x, y = (lax.axis_index(a).astype(jnp.int32) for a in AXES)
    place = jnp.stack([z, c, jnp.where(c == 0, x, y), jnp.where(c == 0, y, x)])
    listed = plan(place, tile_col, tile_slot, mirror_list.reshape(-1), tile_counts)
    up, down = along_z(1), along_z(-1)
    state = features
    for layer in range(LAYERS):
        rows = ROWS + 8 if layer == 0 else ROWS
        if layer == 0:
            gathered, listed = gather(state, listed)
            degree_part = degrees(listed, tiles)
        else:
            gathered, _ = gather(state)
        sent, kept, high, low = products(0, rows, listed, tiles, degree_part, gathered)
        got = send(sent, PAIR)
        sent_mid, kept_mid = products(1, rows, listed, tiles, degree_part, (high, low))
        got, sent_mid, high, low = lax.optimization_barrier((got, sent_mid, high, low))
        got_mid = send(sent_mid, PAIR)
        f, g = send(kept[0] + got[0], up), send(kept[1] + got[1], down)
        sent_last, kept_last = products(2, rows, listed, tiles, degree_part, (high, low))
        f, g, got_mid, sent_last = lax.optimization_barrier((f, g, got_mid, sent_last))
        got_last = send(sent_last, PAIR)
        f = send(f + (kept_mid[0] + got_mid[0]), up)
        g = send(g + (kept_mid[1] + got_mid[1]), down)
        f = send(f + (kept_last[0] + got_last[0]), up)
        g = send(g + (kept_last[1] + got_last[1]), down)
        f = send(f + (kept_last[2] + got_last[2]), up)
        total = f + (g + (kept_last[3] + got_last[3]))
        if layer == 0:
            degree = total[ROWS : ROWS + BLK_DEV, :TILE].reshape(ROWS)
            total = total[:ROWS]
        neighbour_mean = (state + total) / (1.0 + degree)[:, None]
        activated = jax.nn.relu(
            jnp.dot(state, self_weight[layer], precision=lax.Precision.HIGHEST)
            + jnp.dot(neighbour_mean, neigh_weight[layer], precision=lax.Precision.HIGHEST)
        )
        state = activated * lax.rsqrt(jnp.mean(activated * activated, axis=1, keepdims=True) + 1e-05)
    return state


def solution(mesh):
    fine = Mesh(mesh.devices.reshape(NZ, NC, NX, NY), AXES)
    placed = (
        P(AXES, None),
        P(AXES, None, None),
        P(AXES),
        P(AXES),
        P(AXES, None, None),
        P(AXES),
        P(),
        P(),
    )
    return jax.shard_map(body, mesh=fine, in_specs=placed, out_specs=P(AXES, None), check_vma=False)
```

```python
import functools

import jax
import jax.numpy as jnp
from jax import lax
from jax.experimental import pallas as pl
from jax.experimental.pallas import tpu as pltpu
from jax.sharding import Mesh
from jax.sharding import PartitionSpec as P

F = 256
TILE = 128
LAYERS = 2
BLK_DEV = 3
TILES_DEV = 96
CAP = 2
NZ, NC, NX, NY = 8, 2, 4, 4
AXES = ("z", "c", "x", "y")
UNROLL = 8
PIECES = (1, 2, 5)
BASE = (0, 2, 6)
SEGMENTS = len(PIECES)
SLOTS = 2 * TILES_DEV + SEGMENTS * UNROLL
SOURCE, DEST, BOUNDS = SLOTS, 2 * SLOTS, 3 * SLOTS
LISTED = 3 * SLOTS + 8
ROWS = BLK_DEV * TILE
NT = (((1,), (1,)), ((), ()))
BF = jnp.bfloat16
F32 = jnp.float32
VMEM = pl.BlockSpec(memory_space=pltpu.VMEM)
SMEM = pl.BlockSpec(memory_space=pltpu.SMEM)


def perm(step):
    pairs = []
    for z in range(NZ):
        for c in range(NC):
            for x in range(NX):
                for y in range(NY):
                    tz, tc, tx, ty = step(z, c, x, y)
                    pairs.append((
                        ((z * NC + c) * NX + x) * NY + y,
                        (((tz % NZ) * NC + tc % NC) * NX + tx % NX) * NY + ty % NY,
                    ))
    return pairs


PAIR = perm(lambda z, c, x, y: (z, c + 1, x, y))


def along_z(d):
    return perm(lambda z, c, x, y: (z + (d if c == 0 else -d), c, x, y))


def in_plane(d, phase):
    return perm(lambda z, c, x, y: (z, c, x + d, y) if (c + phase) % 2 == 0 else (z, c, x, y + d))


def send(value, pairs):
    return lax.ppermute(value, AXES, pairs)


def split(value):
    high = value.astype(BF)
    return high, (value - high.astype(F32)).astype(BF)


def slot_of(offset):
    return jnp.where(offset == 0, 0, jnp.where(offset == 3, 1, jnp.where(offset == 1, 2, 3)))


def piece_of(r):
    return jnp.where(
        (r == 5) | (r == 6), 1, jnp.where(r == 1, 2, jnp.where(r == 7, 3, jnp.where(r == 0, 4, 0)))
    )


def plan_kernel(place, col, slot, mirror, count, listed, cls, nxt):
    z, c, p, q = place[0], place[1], place[2], place[3]
    for s in range(SEGMENTS + 1):
        nxt[s] = 0

    def classify(t, _):
        sl = slot[t]
        g = sl // CAP
        gz, gc = g // NC, g % NC
        r = lax.bitwise_and(jnp.where(gc == 0, gz - z, z - gz) + NZ, NZ - 1)
        seg = jnp.where(r == 4, 0, jnp.where((r == 3) | (r == 5), 1, 2))
        piece = piece_of(r) + jnp.where(seg == 0, BASE[0], jnp.where(seg == 1, BASE[1], BASE[2]))
        kept = jnp.where(seg == 0, PIECES[0], jnp.where(seg == 1, PIECES[1], PIECES[2]))
        piece += jnp.where(gc == c, kept, 0)
        seg = jnp.where(t < count[0], seg, SEGMENTS)
        cls[t] = seg * 64 + piece * 4 + mirror[sl]
        nxt[seg] = nxt[seg] + 1
        return 0

    lax.fori_loop(0, TILES_DEV, classify, 0)
    start = jnp.int32(0)
    for s in range(SEGMENTS):
        n = nxt[s]
        end = start + (n + UNROLL - 1) // UNROLL * UNROLL
        listed[BOUNDS + s] = start // UNROLL
        nxt[s] = start

        def pad(at, _):
            listed[at] = TILES_DEV
            listed[SOURCE + at] = 0
            listed[DEST + at] = 0
            return 0

        lax.fori_loop(start + n, end, pad, 0)
        start = end
    listed[BOUNDS + SEGMENTS] = start // UNROLL
    nxt[SEGMENTS] = start

    def place_tile(t, _):
        v = cls[t]
        seg = v // 64
        at = nxt[seg]
        nxt[seg] = at + 1
        b = col[t]
        m = b // BLK_DEV
        j = b - m * BLK_DEV
        bx, by = m // NY, m % NY
        sp = slot_of(lax.bitwise_and(jnp.where(c == 0, bx, by) - p + 4, 3))
        sq = slot_of(lax.bitwise_and(jnp.where(c == 0, by, bx) - q + 4, 3))
        listed[at] = t
        listed[SOURCE + at] = sq * 12 + sp * 3 + j
        listed[DEST + at] = v - seg * 64
        return 0

    lax.fori_loop(0, TILES_DEV, place_tile, 0)


def plan(place, col, slot, mirror, count):
    return pl.pallas_call(
        plan_kernel,
        out_shape=jax.ShapeDtypeStruct((LISTED,), jnp.int32),
        in_specs=[SMEM] * 5,
        out_specs=SMEM,
        scratch_shapes=[pltpu.SMEM((TILES_DEV,), jnp.int32), pltpu.SMEM((8,), jnp.int32)],
        cost_estimate=pl.CostEstimate(flops=0, bytes_accessed=2 * 10**7, transcendentals=0),
        name="plan",
    )(place, col, slot, mirror, count)


def tile_at(listed, tiles, s):
    t = listed[s]
    live = (t < TILES_DEV).astype(F32)
    return split(tiles[jnp.minimum(t, TILES_DEV - 1)] * live)


def degree_kernel(listed, tiles, degree):
    degree[...] = jnp.zeros_like(degree)
    ones = jnp.ones((8, TILE), BF)

    def chunk(i, _):
        for u in range(UNROLL):
            s = i * UNROLL + u
            hi, lo = tile_at(listed, tiles, s)
            row = lax.dot_general(ones, hi, NT, preferred_element_type=F32) + lax.dot_general(
                ones, lo, NT, preferred_element_type=F32
            )
            d = listed[DEST + s]
            degree[d // 4, pl.ds(d % 4, 1), :] += row[0:1]
        return 0

    lax.fori_loop(0, listed[BOUNDS + SEGMENTS], chunk, 0)


def degrees(listed, tiles):
    return pl.pallas_call(
        degree_kernel,
        out_shape=jax.ShapeDtypeStruct((2 * NZ, 8, TILE), F32),
        in_specs=[SMEM, VMEM],
        out_specs=VMEM,
        compiler_params=pltpu.CompilerParams(vmem_limit_bytes=16 << 20),
        cost_estimate=pl.CostEstimate(flops=10**8, bytes_accessed=2 * 10**7, transcendentals=0),
        name="degrees",
    )(listed, tiles)


def add_products(stage, rows, listed, tiles, degree, high, low, out):
    places, base = out.shape[0], BASE[stage]

    def clear(i, _):
        out[i] = jnp.zeros((rows, F), F32)
        if rows > ROWS:
            out[i, ROWS:rows, 0:TILE] = degree[base + i]
        return 0

    lax.fori_loop(0, places, clear, 0)

    def chunk(i, _):
        for u in range(UNROLL):
            s = i * UNROLL + u
            b = listed[SOURCE + s]
            hi, lo = tile_at(listed, tiles, s)
            value = jnp.dot(
                jnp.concatenate([hi, lo, hi], axis=1),
                jnp.concatenate([high[b], high[b], low[b]], axis=0),
                preferred_element_type=F32,
            )
            d = listed[DEST + s]
            at = pl.ds(pl.multiple_of(d % 4 * TILE, TILE), TILE)
            out[jnp.maximum(d // 4 - base, 0), at, :] += value
        return 0

    lax.fori_loop(listed[BOUNDS + stage], listed[BOUNDS + stage + 1], chunk, 0)


def first_kernel(rows, listed, tiles, degree, *refs):
    gathered, (out, high, low) = refs[:8], refs[8:]
    blocks = gathered[0].shape[0] // TILE
    for i, ref in enumerate(gathered):

        def load(j, _, i=i, ref=ref):
            at = pl.ds(pl.multiple_of(j * TILE, TILE), TILE)
            high[i * blocks + j], low[i * blocks + j] = split(ref[at, :])
            return 0

        lax.fori_loop(0, blocks, load, 0)
    add_products(0, rows, listed, tiles, degree, high, low, out)


def next_kernel(stage, rows, listed, tiles, degree, high, low, out):
    add_products(stage, rows, listed, tiles, degree, high, low, out)


def products(stage, rows, listed, tiles, degree, sources):
    n = PIECES[stage]
    outs = [jax.ShapeDtypeStruct((2 * n, rows, F), F32)]
    if stage == 0:
        kernel = functools.partial(first_kernel, rows)
        outs += [jax.ShapeDtypeStruct((48, TILE, F), BF)] * 2
    else:
        kernel = functools.partial(next_kernel, stage, rows)
    out, *halves = pl.pallas_call(
        kernel,
        out_shape=tuple(outs),
        in_specs=[SMEM] + [VMEM] * (2 + len(sources)),
        out_specs=(VMEM,) * len(outs),
        compiler_params=pltpu.CompilerParams(vmem_limit_bytes=32 << 20),
        cost_estimate=pl.CostEstimate(flops=10**9 * n, bytes_accessed=n * 40 * 10**5, transcendentals=0),
        name=("early", "mid", "late")[stage],
    )(listed, tiles, degree, *sources)
    return out[:n], out[n:], *halves


def gather(state, meanwhile=None):
    a, b, c = (send(state, in_plane(d, 0)) for d in (1, -1, 2))
    a, b, c, meanwhile = lax.optimization_barrier((a, b, c, meanwhile))
    up, down = in_plane(1, 1), in_plane(-1, 1)
    top, low = jnp.concatenate([state, a], axis=0), jnp.concatenate([b, c], axis=0)
    top, low = lax.optimization_barrier((top, low))
    top_up, top_down = send(top, up), send(top, down)
    low_up, low_down = send(low, up), send(low, down)
    return (top, low, top_up, low_up, top_down, low_down, send(top_up, up), send(low_down, down)), meanwhile


def body(features, tiles, tile_col, tile_slot, mirror_list, tile_counts, self_weight, neigh_weight):
    z, c, x, y = (lax.axis_index(a).astype(jnp.int32) for a in AXES)
    place = jnp.stack([z, c, jnp.where(c == 0, x, y), jnp.where(c == 0, y, x)])
    listed = plan(place, tile_col, tile_slot, mirror_list.reshape(-1), tile_counts)
    up, down = along_z(1), along_z(-1)
    state = features
    for layer in range(LAYERS):
        rows = ROWS + 8 if layer == 0 else ROWS
        if layer == 0:
            gathered, listed = gather(state, listed)
            degree_part = degrees(listed, tiles)
        else:
            gathered, _ = gather(state)
        sent, kept, high, low = products(0, rows, listed, tiles, degree_part, gathered)
        got = send(sent, PAIR)
        sent_mid, kept_mid = products(1, rows, listed, tiles, degree_part, (high, low))
        got, sent_mid, high, low = lax.optimization_barrier((got, sent_mid, high, low))
        got_mid = send(sent_mid, PAIR)
        f = send(kept[0] + got[0], up)
        sent_last, kept_last = products(2, rows, listed, tiles, degree_part, (high, low))
        f, got_mid, sent_last = lax.optimization_barrier((f, got_mid, sent_last))
        got_last = send(sent_last, PAIR)
        f, g = f + (kept_mid[0] + got_mid[0]), kept_mid[1] + got_mid[1]
        f, g = send(f, up), send(g, down)
        p = lax.optimization_barrier(tuple(kept_last[i] + got_last[i] for i in range(5)))
        f, g = send(f + p[0], up), send(g + p[1], down)
        f, g = send(f + p[2], up), send(g + p[3], down)
        total = f + (g + p[4])
        if layer == 0:
            degree = total[ROWS : ROWS + BLK_DEV, :TILE].reshape(ROWS)
            total = total[:ROWS]
        neighbour_mean = (state + total) / (1.0 + degree)[:, None]
        activated = jax.nn.relu(
            jnp.dot(state, self_weight[layer], precision=lax.Precision.HIGHEST)
            + jnp.dot(neighbour_mean, neigh_weight[layer], precision=lax.Precision.HIGHEST)
        )
        state = activated * lax.rsqrt(jnp.mean(activated * activated, axis=1, keepdims=True) + 1e-05)
    return state


def solution(mesh):
    fine = Mesh(mesh.devices.reshape(NZ, NC, NX, NY), AXES)
    placed = (
        P(AXES, None),
        P(AXES, None, None),
        P(AXES),
        P(AXES),
        P(AXES, None, None),
        P(AXES),
        P(),
        P(),
    )
    return jax.shard_map(body, mesh=fine, in_specs=placed, out_specs=P(AXES, None), check_vma=False)
```

```python
import functools

import jax
import jax.numpy as jnp
from jax import lax
from jax.experimental import pallas as pl
from jax.experimental.pallas import tpu as pltpu
from jax.sharding import Mesh
from jax.sharding import PartitionSpec as P

F = 256
TILE = 128
LAYERS = 2
BLK_DEV = 3
TILES_DEV = 96
CAP = 2
NZ, NC, NX, NY = 8, 2, 4, 4
AXES = ("z", "c", "x", "y")
UNROLL = 8
PIECES = (1, 2, 5)
BASE = (0, 2, 6)
SEGMENTS = len(PIECES)
SLOTS = 2 * TILES_DEV + SEGMENTS * UNROLL
SOURCE, DEST, BOUNDS = SLOTS, 2 * SLOTS, 3 * SLOTS
LISTED = 3 * SLOTS + 8
ROWS = BLK_DEV * TILE
NT = (((1,), (1,)), ((), ()))
BF = jnp.bfloat16
F32 = jnp.float32
VMEM = pl.BlockSpec(memory_space=pltpu.VMEM)
SMEM = pl.BlockSpec(memory_space=pltpu.SMEM)


def perm(step):
    pairs = []
    for z in range(NZ):
        for c in range(NC):
            for x in range(NX):
                for y in range(NY):
                    tz, tc, tx, ty = step(z, c, x, y)
                    pairs.append((
                        ((z * NC + c) * NX + x) * NY + y,
                        (((tz % NZ) * NC + tc % NC) * NX + tx % NX) * NY + ty % NY,
                    ))
    return pairs


PAIR = perm(lambda z, c, x, y: (z, c + 1, x, y))


def along_z(d):
    return perm(lambda z, c, x, y: (z + (d if c == 0 else -d), c, x, y))


def in_plane(d, phase):
    return perm(lambda z, c, x, y: (z, c, x + d, y) if (c + phase) % 2 == 0 else (z, c, x, y + d))


def send(value, pairs):
    return lax.ppermute(value, AXES, pairs)


def split(value):
    high = value.astype(BF)
    return high, (value - high.astype(F32)).astype(BF)


def slot_of(offset):
    return jnp.where(offset == 0, 0, jnp.where(offset == 3, 1, jnp.where(offset == 1, 2, 3)))


def piece_of(r):
    return jnp.where(
        (r == 5) | (r == 6), 1, jnp.where(r == 1, 2, jnp.where(r == 7, 3, jnp.where(r == 0, 4, 0)))
    )


def by_fours(step):
    def four(i, _):
        for u in range(4):
            step(i * 4 + u, 0)
        return 0

    lax.fori_loop(0, TILES_DEV // 4, four, 0)


def plan_kernel(place, col, slot, mirror, count, listed, cls, nxt):
    z, c, p, q = place[0], place[1], place[2], place[3]
    for s in range(SEGMENTS + 1):
        nxt[s] = 0

    def classify(t, _):
        sl = slot[t]
        g = sl // CAP
        gz, gc = g // NC, g % NC
        r = lax.bitwise_and(jnp.where(gc == 0, gz - z, z - gz) + NZ, NZ - 1)
        seg = jnp.where(r == 4, 0, jnp.where((r == 3) | (r == 5), 1, 2))
        piece = piece_of(r) + jnp.where(seg == 0, BASE[0], jnp.where(seg == 1, BASE[1], BASE[2]))
        kept = jnp.where(seg == 0, PIECES[0], jnp.where(seg == 1, PIECES[1], PIECES[2]))
        piece += jnp.where(gc == c, kept, 0)
        seg = jnp.where(t < count[0], seg, SEGMENTS)
        cls[t] = seg * 64 + piece * 4 + mirror[sl]
        nxt[seg] = nxt[seg] + 1
        return 0

    by_fours(classify)
    start = jnp.int32(0)
    for s in range(SEGMENTS):
        n = nxt[s]
        end = start + (n + UNROLL - 1) // UNROLL * UNROLL
        listed[BOUNDS + s] = start // UNROLL
        nxt[s] = start

        def pad(at, _):
            listed[at] = TILES_DEV
            listed[SOURCE + at] = 0
            listed[DEST + at] = 0
            return 0

        lax.fori_loop(start + n, end, pad, 0)
        start = end
    listed[BOUNDS + SEGMENTS] = start // UNROLL
    nxt[SEGMENTS] = start

    def place_tile(t, _):
        v = cls[t]
        seg = v // 64
        at = nxt[seg]
        nxt[seg] = at + 1
        b = col[t]
        m = b // BLK_DEV
        j = b - m * BLK_DEV
        bx, by = m // NY, m % NY
        sp = slot_of(lax.bitwise_and(jnp.where(c == 0, bx, by) - p + 4, 3))
        sq = slot_of(lax.bitwise_and(jnp.where(c == 0, by, bx) - q + 4, 3))
        listed[at] = t
        listed[SOURCE + at] = sq * 12 + sp * 3 + j
        listed[DEST + at] = v - seg * 64
        return 0

    by_fours(place_tile)


def plan(place, col, slot, mirror, count):
    return pl.pallas_call(
        plan_kernel,
        out_shape=jax.ShapeDtypeStruct((LISTED,), jnp.int32),
        in_specs=[SMEM] * 5,
        out_specs=SMEM,
        scratch_shapes=[pltpu.SMEM((TILES_DEV,), jnp.int32), pltpu.SMEM((8,), jnp.int32)],
        cost_estimate=pl.CostEstimate(flops=0, bytes_accessed=2 * 10**7, transcendentals=0),
        name="plan",
    )(place, col, slot, mirror, count)


def tile_at(listed, tiles, s):
    t = listed[s]
    live = (t < TILES_DEV).astype(F32)
    return split(tiles[jnp.minimum(t, TILES_DEV - 1)] * live)


def degree_kernel(listed, tiles, degree):
    degree[...] = jnp.zeros_like(degree)
    ones = jnp.ones((8, TILE), BF)

    def chunk(i, _):
        for u in range(UNROLL):
            s = i * UNROLL + u
            hi, lo = tile_at(listed, tiles, s)
            row = lax.dot_general(ones, hi, NT, preferred_element_type=F32) + lax.dot_general(
                ones, lo, NT, preferred_element_type=F32
            )
            d = listed[DEST + s]
            degree[d // 4, pl.ds(d % 4, 1), :] += row[0:1]
        return 0

    lax.fori_loop(0, listed[BOUNDS + SEGMENTS], chunk, 0)


def degrees(listed, tiles):
    return pl.pallas_call(
        degree_kernel,
        out_shape=jax.ShapeDtypeStruct((2 * NZ, 8, TILE), F32),
        in_specs=[SMEM, VMEM],
        out_specs=VMEM,
        compiler_params=pltpu.CompilerParams(vmem_limit_bytes=16 << 20),
        cost_estimate=pl.CostEstimate(flops=10**8, bytes_accessed=2 * 10**7, transcendentals=0),
        name="degrees",
    )(listed, tiles)


def add_products(stage, rows, listed, tiles, degree, high, low, out):
    places, base = out.shape[0], BASE[stage]

    def clear(i, _):
        out[i] = jnp.zeros((rows, F), F32)
        if rows > ROWS:
            out[i, ROWS:rows, 0:TILE] = degree[base + i]
        return 0

    lax.fori_loop(0, places, clear, 0)

    def chunk(i, _):
        for u in range(UNROLL):
            s = i * UNROLL + u
            b = listed[SOURCE + s]
            hi, lo = tile_at(listed, tiles, s)
            value = jnp.dot(
                jnp.concatenate([hi, lo, hi], axis=1),
                jnp.concatenate([high[b], high[b], low[b]], axis=0),
                preferred_element_type=F32,
            )
            d = listed[DEST + s]
            at = pl.ds(pl.multiple_of(d % 4 * TILE, TILE), TILE)
            out[jnp.maximum(d // 4 - base, 0), at, :] += value
        return 0

    lax.fori_loop(listed[BOUNDS + stage], listed[BOUNDS + stage + 1], chunk, 0)


def first_kernel(rows, listed, tiles, degree, *refs):
    gathered, (out, high, low) = refs[:8], refs[8:]
    blocks = gathered[0].shape[0] // TILE
    for i, ref in enumerate(gathered):

        def load(j, _, i=i, ref=ref):
            at = pl.ds(pl.multiple_of(j * TILE, TILE), TILE)
            high[i * blocks + j], low[i * blocks + j] = split(ref[at, :])
            return 0

        lax.fori_loop(0, blocks, load, 0)
    add_products(0, rows, listed, tiles, degree, high, low, out)


def next_kernel(stage, rows, listed, tiles, degree, high, low, out):
    add_products(stage, rows, listed, tiles, degree, high, low, out)


def products(stage, rows, listed, tiles, degree, sources):
    n = PIECES[stage]
    outs = [jax.ShapeDtypeStruct((2 * n, rows, F), F32)]
    if stage == 0:
        kernel = functools.partial(first_kernel, rows)
        outs += [jax.ShapeDtypeStruct((48, TILE, F), BF)] * 2
    else:
        kernel = functools.partial(next_kernel, stage, rows)
    out, *halves = pl.pallas_call(
        kernel,
        out_shape=tuple(outs),
        in_specs=[SMEM] + [VMEM] * (2 + len(sources)),
        out_specs=(VMEM,) * len(outs),
        compiler_params=pltpu.CompilerParams(vmem_limit_bytes=32 << 20),
        cost_estimate=pl.CostEstimate(flops=10**9 * n, bytes_accessed=n * 40 * 10**5, transcendentals=0),
        name=("early", "mid", "late")[stage],
    )(listed, tiles, degree, *sources)
    return out[:n], out[n:], *halves


def gather(state, meanwhile=None):
    c, a, b = (send(state, in_plane(d, 0)) for d in (2, 1, -1))
    a, b, c, meanwhile = lax.optimization_barrier((a, b, c, meanwhile))
    up, down = in_plane(1, 1), in_plane(-1, 1)
    top, low = jnp.concatenate([state, a], axis=0), jnp.concatenate([b, c], axis=0)
    top, low = lax.optimization_barrier((top, low))
    top_up, top_down = send(top, up), send(top, down)
    low_up, low_down = send(low, up), send(low, down)
    return (top, low, top_up, low_up, top_down, low_down, send(top_up, up), send(low_down, down)), meanwhile


def body(features, tiles, tile_col, tile_slot, mirror_list, tile_counts, self_weight, neigh_weight):
    z, c, x, y = (lax.axis_index(a).astype(jnp.int32) for a in AXES)
    place = jnp.stack([z, c, jnp.where(c == 0, x, y), jnp.where(c == 0, y, x)])
    listed = plan(place, tile_col, tile_slot, mirror_list.reshape(-1), tile_counts)
    up, down = along_z(1), along_z(-1)
    state = features
    for layer in range(LAYERS):
        rows = ROWS + 8 if layer == 0 else ROWS
        if layer == 0:
            gathered, listed = gather(state, listed)
            degree_part = degrees(listed, tiles)
        else:
            gathered, _ = gather(state)
        sent, kept, high, low = products(0, rows, listed, tiles, degree_part, gathered)
        got = send(sent, PAIR)
        sent_mid, kept_mid = products(1, rows, listed, tiles, degree_part, (high, low))
        got, sent_mid, high, low = lax.optimization_barrier((got, sent_mid, high, low))
        got_mid = send(sent_mid, PAIR)
        f = send(kept[0] + got[0], up)
        sent_last, kept_last = products(2, rows, listed, tiles, degree_part, (high, low))
        f, got_mid, sent_last = lax.optimization_barrier((f, got_mid, sent_last))
        got_last = send(sent_last, PAIR)
        f, g = f + (kept_mid[0] + got_mid[0]), kept_mid[1] + got_mid[1]
        f, g = send(f, up), send(g, down)
        p = lax.optimization_barrier(tuple(kept_last[i] + got_last[i] for i in range(5)))
        f, g = send(f + p[0], up), send(g + p[1], down)
        f, g = send(f + p[2], up), send(g + p[3], down)
        total = f + (g + p[4])
        if layer == 0:
            degree = total[ROWS : ROWS + BLK_DEV, :TILE].reshape(ROWS)
            total = total[:ROWS]
        neighbour_mean = (state + total) / (1.0 + degree)[:, None]
        activated = jax.nn.relu(
            jnp.dot(state, self_weight[layer], precision=lax.Precision.HIGHEST)
            + jnp.dot(neighbour_mean, neigh_weight[layer], precision=lax.Precision.HIGHEST)
        )
        state = activated * lax.rsqrt(jnp.mean(activated * activated, axis=1, keepdims=True) + 1e-05)
    return state


def solution(mesh):
    fine = Mesh(mesh.devices.reshape(NZ, NC, NX, NY), AXES)
    placed = (
        P(AXES, None),
        P(AXES, None, None),
        P(AXES),
        P(AXES),
        P(AXES, None, None),
        P(AXES),
        P(),
        P(),
    )
    return jax.shard_map(body, mesh=fine, in_specs=placed, out_specs=P(AXES, None), check_vma=False)
```
